32 devices in a mesh: aa: 8 (over z, x), ba: 4 (over y, core).
Axes of the slice: x: 2, y: 2, z: 4, core: 2. Of those that a mesh axis runs over, the one named last changes fastest.
Arguments:
- grid_fields: bfloat16 [1920, 36, 3072], P('aa', None, 'ba'), may hold values from -6 to 6
- band_rows: int32 [8], replicated, may hold values from 1 to 240, 1280 in all
- wave_owner: int32 [640], replicated, may hold values from 0 to 639, each once
- lower_blocks: float32 [3, 3, 12], replicated, may hold values from -0.3 to 0.3
- pivot_inverse: float32 [3, 3, 12], replicated, may hold values from -0.2 to 1.1, as said below
- upper_blocks: float32 [3, 3, 12], replicated, may hold values from -0.3 to 0.3
- legendre: bfloat16 [640, 1280, 896], P(('aa', 'ba')), may hold values from -0.0029296875 to 0.0029296875
Outputs:
- spectral: float32 [640, 72, 896], P(('aa', 'ba'))
The draws below stay inside these ranges and needn't reach their ends.
Inputs may be any that keep to these rules, and one draw needn't show every extreme that they name: The latitudes of band d fill its first band_rows[d] row slots in order; the bands' counts add up to 1280; row slots past a band's count are never read. `wave_owner`: each wavenumber 0 to 639 appears once. `pivot_inverse`: diagonal entries lie in 0.6 to 1.1, the others within -0.2 to 0.2.
All inputs are finite; a program needn't handle non-finite values.
Results may differ from the reference program's by a relative error of at most 0.0047.
Values may be sent and summed in bfloat16 or wider, within the bound.
A program may use at most 192 MiB of HBM per device.

```python
import math
import jax
import jax.numpy as jnp
import numpy as np
from jax import lax

LEV = 12
FIELDS = 3
NLON = 3072
NLAT = 1280
M = 640
NDEG = 896
NT = 1279
RMAX = 240
SLOTS = 1920
N_AA = 8


def draw_pivot_inverse(key, part):
    key_diag, key_off = jax.random.split(jax.random.fold_in(key, 11))
    diagonal = jax.random.uniform(key_diag, (FIELDS, LEV), jnp.float32, 0.6, 1.1)
    others = jax.random.uniform(key_off, (FIELDS, FIELDS, LEV), jnp.float32, -0.2, 0.2)
    identity = jnp.eye(FIELDS, dtype=jnp.float32)[:, :, None]
    return others * (1.0 - identity) + identity * diagonal[:, None, :]


def level_of(own_key, shape, pieces, smallest, top_value):
    def one(position, shards_of):
        draws = jax.random.uniform(jax.random.fold_in(jax.random.fold_in(own_key, 6), position), (shards_of,), jnp.float32, smallest / len(pieces), top_value / len(pieces))
        return jnp.repeat(jnp.exp(draws), shape[position] // shards_of).reshape((-1,) + (1,) * (len(shape) - position - 1))

    level = one(*pieces[0])
    for cut in pieces[1:]:
        level = level * one(*cut)
    return level


def length_profile(count, total, limit, slope):
    weights = [(1 << 20) // math.isqrt(standing ** slope) + 1 for standing in range(2, count + 1)]
    spare, holding = total - limit - (count - 1), [1] * (count - 1)
    while spare > 0:
        movable = [i for i in range(count - 1) if holding[i] < limit]
        pool, left = sum([weights[i] for i in movable]), spare
        for i in movable:
            more = min(limit - holding[i], max(1, left * weights[i] // pool), spare)
            holding[i] = holding[i] + more
            spare = spare - more
    return np.array([limit] + holding)


def ragged(own_key, number_of, total, most, lean):
    if number_of == 2:
        one = jax.random.randint(own_key, (), max(1, total - most), min(most, total - 1) + 1)
        return jnp.stack([one, total - one])
    lengths = jnp.asarray(length_profile(number_of, total, most, lean), jnp.int32)
    couples = (number_of - 1) // 2
    donor, receiver = lengths[1:1 + 2 * couples:2], lengths[2:2 + 2 * couples:2]
    room = jnp.minimum(donor - 1, most - receiver)
    shifted = jax.random.randint(jax.random.fold_in(own_key, 1), (couples,), 0, 1 << 20) % (room + 1)
    lengths = lengths.at[1:1 + 2 * couples:2].set(donor - shifted).at[2:2 + 2 * couples:2].set(receiver + shifted)
    return lengths[jax.random.permutation(jax.random.fold_in(own_key, 2), number_of)]


def normal_values(own_key, shape, scale, most, cuts=(), kind=jnp.bfloat16):
    entries = jax.random.normal(own_key, shape, jnp.float32) * scale
    if len(cuts) > 0:
        entries = level_of(own_key, shape, cuts, -0.22, 0.18) * entries
    return jnp.clip(entries, min=-most, max=most).astype(kind)


def setup_inputs(seed: int = 0) -> dict:
    splits = jax.random.split(jax.random.key(seed), 8)
    grid_fields = normal_values(splits[0], (SLOTS, FIELDS * LEV, NLON), 1.0, 6.0, ((0, 8), (2, 4)))
    band_rows = ragged(splits[1], N_AA, NLAT, RMAX, 2).astype(jnp.int32)
    wave_owner = jax.random.permutation(splits[2], M).astype(jnp.int32)
    lower_blocks = jnp.clip(jax.random.uniform(splits[3], (FIELDS, FIELDS, LEV), jnp.float32, -0.3, 0.3), -0.3, 0.3)
    pivot_inverse = draw_pivot_inverse(jax.random.fold_in(splits[7], 71), 0)
    upper_blocks = jnp.clip(jax.random.uniform(splits[5], (FIELDS, FIELDS, LEV), jnp.float32, -0.3, 0.3), -0.3, 0.3)
    legendre = normal_values(splits[6], (M, NLAT, NDEG), (NLAT * NLON) ** -0.5, 0.0029296875, ((0, 32),))
    return dict(grid_fields=grid_fields, band_rows=band_rows, wave_owner=wave_owner, lower_blocks=lower_blocks, pivot_inverse=pivot_inverse, upper_blocks=upper_blocks, legendre=legendre)


def apply_block(block, vector):
    width = vector.shape[1]
    outputs = []
    for row_index in range(width):
        total = block[row_index, 0] * vector[:, 0]
        for col_index in range(1, width):
            total = total + block[row_index, col_index] * vector[:, col_index]
        outputs.append(total)
    return jnp.stack(outputs, axis=1)


def block_product(left_blocks, right_blocks):
    width = left_blocks.shape[0]
    rows_out = []
    for row_index in range(width):
        cols_out = []
        for col_index in range(width):
            total = left_blocks[row_index, 0] * right_blocks[0, col_index]
            for inner in range(1, width):
                total = total + left_blocks[row_index, inner] * right_blocks[inner, col_index]
            cols_out.append(total)
        rows_out.append(jnp.stack(cols_out, axis=0))
    return jnp.stack(rows_out, axis=0)


def diffuse(band, lower_blocks, pivot_inverse, upper_blocks):
    slot_rows, lf_total, lon_width = band.shape
    levels = lower_blocks.shape[2]
    fields = lf_total // levels
    values = band.astype(jnp.float32).reshape(slot_rows, fields, levels, lon_width)
    values = jnp.moveaxis(values, 2, 0)
    coupling = block_product(pivot_inverse, upper_blocks)
    lower_seq = jnp.moveaxis(lower_blocks, 2, 0)
    inverse_seq = jnp.moveaxis(pivot_inverse, 2, 0)
    coupling_seq = jnp.moveaxis(coupling, 2, 0)

    def forward(carry, inputs):
        source, lower_lev, inverse_lev = inputs
        sweep = apply_block(inverse_lev, source - apply_block(lower_lev, carry))
        return sweep, sweep

    zero_state = jnp.zeros(values.shape[1:], jnp.float32)
    last_sweep, sweeps = lax.scan(forward, zero_state, (values, lower_seq, inverse_seq))

    def backward(carry, inputs):
        sweep, coupling_lev = inputs
        result = sweep - apply_block(coupling_lev, carry)
        return result, result

    last_solved, solved = lax.scan(backward, zero_state, (sweeps, coupling_seq), reverse=True)
    solved = jnp.moveaxis(solved, 0, 2).reshape(slot_rows, lf_total, lon_width)
    return solved.astype(jnp.bfloat16)


def fourier_table(wave_owner, lon_total):
    lon_index = jnp.arange(lon_total, dtype=jnp.int32)
    phase = (wave_owner.astype(jnp.int32)[:, None] * lon_index[None, :]) % lon_total
    angle = phase.astype(jnp.float32) * (2.0 * math.pi / lon_total)
    return jnp.stack([jnp.cos(angle), -jnp.sin(angle)]).astype(jnp.bfloat16)


def latitude_slots(band_rows, slot_rows, lat_total):
    counts = band_rows.astype(jnp.int32)
    band_ends = jnp.cumsum(counts).astype(jnp.int32)
    starts = band_ends - counts
    latitude = jnp.arange(lat_total, dtype=jnp.int32)
    band_index = jnp.sum((band_ends[None, :] <= latitude[:, None]).astype(jnp.int32), axis=1).astype(jnp.int32)
    in_band = band_index[:, None] == jnp.arange(counts.shape[0], dtype=jnp.int32)[None, :]
    band_start = jnp.sum(jnp.where(in_band, starts[None, :], 0), axis=1).astype(jnp.int32)
    return (band_index * slot_rows + latitude - band_start).astype(jnp.int32)


def reference(grid_fields, band_rows, wave_owner, lower_blocks, pivot_inverse, upper_blocks, legendre):
    slot_rows = grid_fields.shape[0] // N_AA
    lf_total = FIELDS * LEV
    flat_table = fourier_table(wave_owner, NLON).reshape(2 * M, NLON)

    def transform(band):
        smooth = diffuse(band, lower_blocks, pivot_inverse, upper_blocks)
        flat_rows = smooth.reshape(slot_rows * lf_total, NLON)
        fourier = jnp.dot(flat_table, flat_rows.T, preferred_element_type=jnp.float32)
        return fourier.astype(jnp.bfloat16).reshape(2, M, slot_rows, lf_total)

    bands = grid_fields.reshape(N_AA, slot_rows, lf_total, NLON)
    fourier = lax.map(transform, bands)
    panels = jnp.transpose(fourier, (2, 1, 4, 0, 3)).reshape(M, 2 * lf_total, N_AA * slot_rows)
    lat_slot = latitude_slots(band_rows, slot_rows, NLAT)
    panels = jnp.take(panels, lat_slot, axis=2)
    degree = jnp.arange(NDEG, dtype=jnp.int32)

    def project(inputs):
        panel, table_rows, owner = inputs
        coef = jnp.dot(panel, table_rows, preferred_element_type=jnp.float32)
        return jnp.where((degree + owner <= NT)[None, :], coef, 0.0)

    return lax.map(project, (panels, legendre, wave_owner.astype(jnp.int32)))
```

```python
import functools
import math

import jax
import jax.numpy as jnp
import numpy as np
from jax import lax
from jax.experimental import pallas as pl
from jax.experimental.pallas import tpu as pltpu
from jax.sharding import PartitionSpec as P

NT = 1279
CHUNKS = 6
VMEM = 48 * 1024 * 1024


def params():
    return pltpu.CompilerParams(vmem_limit_bytes=VMEM)


def angle(phase, lon_total):
    return phase.astype(jnp.float32) * (2.0 * math.pi / lon_total)


def table_kernel(base_ref, step_ref, out_ref, *, lon_total):
    base = angle(base_ref[...], lon_total)
    step = angle(step_ref[...], lon_total)
    cos_a, sin_a = jnp.cos(base), jnp.sin(base)
    cos_b, sin_b = jnp.cos(step), jnp.sin(step)
    for block in range(out_ref.shape[1] // 128):
        one = slice(block, block + 1)
        out_ref[:, block * 128:(block + 1) * 128] = (
            cos_a[:, one] * cos_b - sin_a[:, one] * sin_b
        ).astype(jnp.bfloat16)


def make_table(waves, quadrant, first_lon, lon_count, lon_total):
    rows = waves.shape[0]
    blocks = lon_count // 128
    starts = first_lon + 128 * jnp.arange(128, dtype=jnp.int32)
    base = (waves[:, None] * starts[None, :] + quadrant[:, None] * (lon_total // 4)) % lon_total
    step = (waves[:, None] * jnp.arange(128, dtype=jnp.int32)[None, :]) % lon_total
    tile = rows // 8 if rows % 64 == 0 else rows
    return pl.pallas_call(
        functools.partial(table_kernel, lon_total=lon_total),
        grid=(rows // tile,),
        in_specs=[pl.BlockSpec((tile, 128), lambda i: (i, 0))] * 2,
        out_specs=pl.BlockSpec((tile, blocks * 128), lambda i: (i, 0)),
        out_shape=jax.ShapeDtypeStruct((rows, blocks * 128), jnp.bfloat16),
        compiler_params=params(),
        name="table",
    )(base, step)


NN = (((1,), (1,)), ((), ()))


def dft_kernel(table_ref, grid_ref, *rest):
    out_ref = rest[-1]
    width = grid_ref.shape[3]
    dests, _, rows, _ = out_ref.shape
    total = lax.dot_general(table_ref[:, :width], grid_ref[0, 0], NN, preferred_element_type=jnp.float32)
    total += lax.dot_general(table_ref[:, width:], grid_ref[1, 0], NN, preferred_element_type=jnp.float32)
    for dest in range(dests):
        piece = total[dest * rows:(dest + 1) * rows]
        if len(rest) == 2:
            piece = piece + rest[0][dest, 0].astype(jnp.float32)
        out_ref[dest, 0] = piece.astype(jnp.bfloat16)


def dft(table, grid, first, count, dests, more=None):
    rows = table.shape[0] // dests
    slots = grid.shape[2]
    out_spec = pl.BlockSpec((dests, 1, rows, slots), lambda i: (0, i, 0, 0))
    in_specs = [
        pl.BlockSpec(table.shape, lambda i: (0, 0)),
        pl.BlockSpec((2, 1) + grid.shape[2:], lambda i: (0, first + i, 0, 0)),
    ]
    operands = [table, grid]
    if more is not None:
        in_specs.append(out_spec)
        operands.append(more)
    flops = 2 * table.shape[0] * table.shape[1] * slots * count
    return pl.pallas_call(
        dft_kernel,
        grid=(count,),
        in_specs=in_specs,
        out_specs=out_spec,
        out_shape=jax.ShapeDtypeStruct((dests, count, rows, slots), jnp.bfloat16),
        compiler_params=params(),
        cost_estimate=pl.CostEstimate(flops=flops, bytes_accessed=table.size * 2 + count * slots * 6000, transcendentals=0),
        name="dft",
    )(*operands)


def place_kernel(place_ref, in_ref, out_ref):
    bands, _, count, rows, slots = in_ref.shape
    for q in range(count):
        total = jnp.dot(in_ref[0, 0, q], place_ref[0], preferred_element_type=jnp.float32)
        for band in range(1, bands):
            total += jnp.dot(in_ref[band, 0, q], place_ref[band], preferred_element_type=jnp.float32)
        out_ref[0, q] = total.astype(jnp.bfloat16)


def place_rows(place, arrived):
    bands, pair, count, rows, slots = arrived.shape
    lats = place.shape[2]
    flops = 2 * pair * count * rows * bands * slots * lats
    return pl.pallas_call(
        place_kernel,
        grid=(pair,),
        in_specs=[
            pl.BlockSpec(place.shape, lambda i: (0, 0, 0)),
            pl.BlockSpec((bands, 1, count, rows, slots), lambda i: (0, i, 0, 0, 0)),
        ],
        out_specs=pl.BlockSpec((1, count, rows, lats), lambda i: (i, 0, 0, 0)),
        out_shape=jax.ShapeDtypeStruct((pair, count, rows, lats), jnp.bfloat16),
        compiler_params=params(),
        cost_estimate=pl.CostEstimate(flops=flops, bytes_accessed=place.size * 2, transcendentals=0),
        name="place",
    )(place, arrived)


def solve_kernel(lower_ref, inverse_ref, upper_ref, out_ref, *, fields, levels):
    lane = lax.broadcasted_iota(jnp.int32, (1, 128), 1)
    cut = lambda ref, a, b, k: ref[(a * fields + b) * levels + k]

    def apply(ref, k, vector):
        return [sum(cut(ref, a, b, k) * vector[b] for b in range(fields)) for a in range(fields)]

    state = [jnp.zeros((1, 128), jnp.float32) for _ in range(fields)]
    sweeps = []
    for k in range(levels):
        low = apply(lower_ref, k, state)
        source = [(lane == f * levels + k).astype(jnp.float32) - low[f] for f in range(fields)]
        state = apply(inverse_ref, k, source)
        sweeps.append(state)
    state = [jnp.zeros((1, 128), jnp.float32) for _ in range(fields)]
    for k in range(levels - 1, -1, -1):
        back = apply(inverse_ref, k, apply(upper_ref, k, state))
        state = [sweeps[k][f] - back[f] for f in range(fields)]
        for f in range(fields):
            out_ref[f * levels + k:f * levels + k + 1, :] = state[f]


def vertical_operator(lower_blocks, pivot_inverse, upper_blocks):
    fields, _, levels = lower_blocks.shape
    whole = pl.pallas_call(
        functools.partial(solve_kernel, fields=fields, levels=levels),
        in_specs=[pl.BlockSpec(memory_space=pltpu.SMEM)] * 3,
        out_specs=pl.BlockSpec(memory_space=pltpu.VMEM),
        out_shape=jax.ShapeDtypeStruct((fields * levels, 128), jnp.float32),
        name="vertical",
    )(lower_blocks.reshape(-1), pivot_inverse.reshape(-1), upper_blocks.reshape(-1))
    return whole[:, :fields * levels]


def legendre_kernel(owner_ref, mix_ref, panel_ref, legendre_ref, out_ref):
    slot = pl.program_id(0)
    total = jnp.dot(panel_ref[0], legendre_ref[0], preferred_element_type=jnp.float32)
    high = total.astype(jnp.bfloat16)
    low = (total - high.astype(jnp.float32)).astype(jnp.bfloat16)
    count = total.shape[0]
    mixed = jnp.dot(mix_ref[0], high, preferred_element_type=jnp.float32)
    mixed += jnp.dot(mix_ref[0], low, preferred_element_type=jnp.float32)
    mixed += jnp.dot(mix_ref[1], high, preferred_element_type=jnp.float32)
    degree = lax.broadcasted_iota(jnp.int32, mixed.shape, 1)
    out_ref[0] = jnp.where(degree + owner_ref[slot] <= NT, mixed, 0.0)


def project(owners, mix, panels, legendre):
    slots, rows, lats = panels.shape
    degrees = legendre.shape[2]
    return pl.pallas_call(
        legendre_kernel,
        grid=(slots,),
        in_specs=[
            pl.BlockSpec(memory_space=pltpu.SMEM),
            pl.BlockSpec(mix.shape, lambda i: (0, 0, 0)),
            pl.BlockSpec((1, rows, lats), lambda i: (i, 0, 0)),
            pl.BlockSpec((1, lats, degrees), lambda i: (i, 0, 0)),
        ],
        out_specs=pl.BlockSpec((1, rows, degrees), lambda i: (i, 0, 0)),
        out_shape=jax.ShapeDtypeStruct((slots, rows, degrees), jnp.float32),
        compiler_params=params(),
        name="legendre",
    )(owners, mix, panels, legendre)


def shards(bands, pairs, grid_fields, band_rows, wave_owner, lower_blocks, pivot_inverse, upper_blocks, legendre):
    slot_rows, columns, lons = grid_fields.shape
    lon_total = lons * 2 * pairs
    per, lats, _ = legendre.shape
    a, b = lax.axis_index("aa"), lax.axis_index("ba")
    side = b // 2
    half = columns // 2
    group = 2 * pairs

    grid = jnp.transpose(grid_fields, (1, 0, 2)).reshape(2, half, slot_rows, lons)
    duos = [[2 * y, 2 * y + 1] for y in range(pairs)]
    grid = lax.all_to_all(grid, "ba", split_axis=0, concat_axis=0, axis_index_groups=duos, tiled=True)

    owners = wave_owner.reshape(bands, pairs, 2, per)
    pad = -(2 * per) % 8
    rows = 2 * per + pad

    def side_rows(which):
        mine = lax.dynamic_index_in_dim(owners, which, 1, keepdims=False)
        waves = jnp.concatenate([mine, mine], axis=2)
        return jnp.pad(waves, ((0, 0), (0, 0), (0, pad))).reshape(-1)

    quadrant = jnp.asarray(np.tile(np.repeat(np.arange(2), per).tolist() + [0] * pad, bands * 2), jnp.int32)
    tables = [make_table(side_rows(w), quadrant, side * 2 * lons, 2 * lons, lon_total) for w in (1 - side, side)]

    ends = jnp.cumsum(band_rows)
    slot = jnp.arange(slot_rows, dtype=jnp.int32)
    target = jnp.where(slot[None, :] < band_rows[:, None], (ends - band_rows)[:, None] + slot[None, :], -1)
    place = (target[:, :, None] == jnp.arange(lats, dtype=jnp.int32)).astype(jnp.bfloat16)

    dests = 2 * bands
    count = half // CHUNKS
    across = [(2 * y + c, 2 * (1 - y) + c) for y in range(2) for c in range(2)]
    teams = [[aa * group + 2 * y + c for aa in range(bands) for c in range(2)] for y in range(pairs)]
    sent = []
    for chunk in range(CHUNKS):
        part = dft(tables[0], grid, chunk * count, count, dests)
        sent.append(lax.ppermute(part, "ba", across))
    placed = []
    for chunk in range(CHUNKS):
        full = dft(tables[1], grid, chunk * count, count, dests, sent[chunk])
        arrived = lax.all_to_all(full, ("aa", "ba"), split_axis=0, concat_axis=0, axis_index_groups=teams, tiled=True)
        placed.append(place_rows(place, arrived.reshape(bands, 2, count, rows, slot_rows)))
    panels = jnp.stack(placed, axis=1)[:, :, :, :2 * per].reshape(columns, 2, per, lats)
    panels = jnp.transpose(panels, (2, 1, 0, 3)).reshape(per, 2 * columns, lats)

    operator = vertical_operator(lower_blocks, pivot_inverse, upper_blocks)
    mix = jnp.kron(jnp.eye(2, dtype=jnp.float32), operator)
    high = mix.astype(jnp.bfloat16)
    low = (mix - high.astype(jnp.float32)).astype(jnp.bfloat16)
    mine = lax.dynamic_slice_in_dim(wave_owner, (a * group + b) * per, per)
    return project(mine, jnp.stack([high, low]), panels, legendre)


def solution(mesh):
    bands, group = mesh.shape["aa"], mesh.shape["ba"]
    placed = (P("aa", None, "ba"), P(), P(), P(), P(), P(), P(("aa", "ba"), None, None))
    return jax.shard_map(
        functools.partial(shards, bands, group // 2),
        mesh=mesh, in_specs=placed, out_specs=P(("aa", "ba"), None, None), check_vma=False,
    )
```

```python
import functools
import math

import jax
import jax.numpy as jnp
import numpy as np
from jax import lax
from jax.experimental import pallas as pl
from jax.experimental.pallas import tpu as pltpu
from jax.sharding import PartitionSpec as P

NT = 1279
CHUNKS = 6
VMEM = 48 * 1024 * 1024


def params():
    return pltpu.CompilerParams(vmem_limit_bytes=VMEM)


def angle(phase, lon_total):
    return phase.astype(jnp.float32) * (2.0 * math.pi / lon_total)


def table_kernel(base_ref, step_ref, out_ref, *, lon_total):
    base = angle(base_ref[...], lon_total)
    step = angle(step_ref[...], lon_total)
    cos_a, sin_a = jnp.cos(base), jnp.sin(base)
    cos_b, sin_b = jnp.cos(step), jnp.sin(step)
    for block in range(out_ref.shape[1] // 128):
        one = slice(block, block + 1)
        out_ref[:, block * 128:(block + 1) * 128] = (
            cos_a[:, one] * cos_b - sin_a[:, one] * sin_b
        ).astype(jnp.bfloat16)


def make_table(waves, quadrant, first_lon, lon_count, lon_total):
    rows = waves.shape[0]
    blocks = lon_count // 128
    starts = first_lon + 128 * jnp.arange(128, dtype=jnp.int32)
    base = (waves[:, None] * starts[None, :] + quadrant[:, None] * (lon_total // 4)) % lon_total
    step = (waves[:, None] * jnp.arange(128, dtype=jnp.int32)[None, :]) % lon_total
    tile = rows // 8 if rows % 64 == 0 else rows
    return pl.pallas_call(
        functools.partial(table_kernel, lon_total=lon_total),
        grid=(rows // tile,),
        in_specs=[pl.BlockSpec((tile, 128), lambda i: (i, 0))] * 2,
        out_specs=pl.BlockSpec((tile, blocks * 128), lambda i: (i, 0)),
        out_shape=jax.ShapeDtypeStruct((rows, blocks * 128), jnp.bfloat16),
        compiler_params=params(),
        name="table",
    )(base, step)


NN = (((1,), (1,)), ((), ()))


def dft_kernel(table_ref, grid_ref, *rest):
    out_ref = rest[-1]
    width = grid_ref.shape[3]
    dests, _, rows, _ = out_ref.shape
    total = lax.dot_general(table_ref[:, :width], grid_ref[0, 0], NN, preferred_element_type=jnp.float32)
    total += lax.dot_general(table_ref[:, width:], grid_ref[1, 0], NN, preferred_element_type=jnp.float32)
    for dest in range(dests):
        piece = total[dest * rows:(dest + 1) * rows]
        if len(rest) == 2:
            piece = piece + rest[0][dest, 0].astype(jnp.float32)
        out_ref[dest, 0] = piece.astype(jnp.bfloat16)


def dft(table, grid, first, count, dests, more=None):
    rows = table.shape[0] // dests
    slots = grid.shape[2]
    out_spec = pl.BlockSpec((dests, 1, rows, slots), lambda i: (0, i, 0, 0))
    in_specs = [
        pl.BlockSpec(table.shape, lambda i: (0, 0)),
        pl.BlockSpec((2, 1) + grid.shape[2:], lambda i: (0, first + i, 0, 0)),
    ]
    operands = [table, grid]
    if more is not None:
        in_specs.append(out_spec)
        operands.append(more)
    flops = 2 * table.shape[0] * table.shape[1] * slots * count
    return pl.pallas_call(
        dft_kernel,
        grid=(count,),
        in_specs=in_specs,
        out_specs=out_spec,
        out_shape=jax.ShapeDtypeStruct((dests, count, rows, slots), jnp.bfloat16),
        compiler_params=params(),
        cost_estimate=pl.CostEstimate(flops=flops, bytes_accessed=table.size * 2 + count * slots * 6000, transcendentals=0),
        name="dft",
    )(*operands)


def place_kernel(place_ref, order_ref, in_ref, out_ref):
    bands = in_ref.shape[0]
    slots, width, lats = out_ref.shape
    total = jnp.zeros((slots * width, lats), jnp.float32)
    for band in range(bands):
        ordered = jnp.dot(order_ref[...], in_ref[band], preferred_element_type=jnp.float32)
        total += jnp.dot(ordered.astype(jnp.bfloat16), place_ref[band], preferred_element_type=jnp.float32)
    out_ref[...] = total.astype(jnp.bfloat16).reshape(slots, width, lats)


def place_rows(place, order, arrived, slots):
    bands, rows, slot_rows = arrived.shape
    lats = place.shape[2]
    flops = 2 * order.shape[0] * bands * slot_rows * lats
    return pl.pallas_call(
        place_kernel,
        out_shape=jax.ShapeDtypeStruct((slots, order.shape[0] // slots, lats), jnp.bfloat16),
        in_specs=[pl.BlockSpec(memory_space=pltpu.VMEM)] * 3,
        out_specs=pl.BlockSpec(memory_space=pltpu.VMEM),
        compiler_params=params(),
        cost_estimate=pl.CostEstimate(flops=2 * flops, bytes_accessed=place.size * 2, transcendentals=0),
        name="place",
    )(place, order, arrived)


def solve_kernel(lower_ref, inverse_ref, upper_ref, out_ref, *, fields, levels):
    lane = lax.broadcasted_iota(jnp.int32, (1, 128), 1)
    cut = lambda ref, a, b, k: ref[(a * fields + b) * levels + k]

    def apply(ref, k, vector):
        return [sum(cut(ref, a, b, k) * vector[b] for b in range(fields)) for a in range(fields)]

    state = [jnp.zeros((1, 128), jnp.float32) for _ in range(fields)]
    sweeps = []
    for k in range(levels):
        low = apply(lower_ref, k, state)
        source = [(lane == f * levels + k).astype(jnp.float32) - low[f] for f in range(fields)]
        state = apply(inverse_ref, k, source)
        sweeps.append(state)
    state = [jnp.zeros((1, 128), jnp.float32) for _ in range(fields)]
    for k in range(levels - 1, -1, -1):
        back = apply(inverse_ref, k, apply(upper_ref, k, state))
        state = [sweeps[k][f] - back[f] for f in range(fields)]
        for f in range(fields):
            out_ref[f * levels + k:f * levels + k + 1, :] = state[f]


def vertical_operator(lower_blocks, pivot_inverse, upper_blocks):
    fields, _, levels = lower_blocks.shape
    whole = pl.pallas_call(
        functools.partial(solve_kernel, fields=fields, levels=levels),
        in_specs=[pl.BlockSpec(memory_space=pltpu.SMEM)] * 3,
        out_specs=pl.BlockSpec(memory_space=pltpu.VMEM),
        out_shape=jax.ShapeDtypeStruct((fields * levels, 128), jnp.float32),
        name="vertical",
    )(lower_blocks.reshape(-1), pivot_inverse.reshape(-1), upper_blocks.reshape(-1))
    return whole[:, :fields * levels]


def legendre_kernel(owner_ref, mix_ref, legendre_ref, *rest):
    out_ref = rest[-1]
    slot = pl.program_id(0)
    panel = jnp.concatenate([ref[0] for ref in rest[:-1]], axis=0)
    total = jnp.dot(panel, legendre_ref[0], preferred_element_type=jnp.float32)
    high = total.astype(jnp.bfloat16)
    low = (total - high.astype(jnp.float32)).astype(jnp.bfloat16)
    mixed = jnp.dot(mix_ref[0], high, preferred_element_type=jnp.float32)
    mixed += jnp.dot(mix_ref[0], low, preferred_element_type=jnp.float32)
    mixed += jnp.dot(mix_ref[1], high, preferred_element_type=jnp.float32)
    degree = lax.broadcasted_iota(jnp.int32, mixed.shape, 1)
    out_ref[0] = jnp.where(degree + owner_ref[slot] <= NT, mixed, 0.0)


def project(owners, mix, panels, legendre):
    slots, width, lats = panels[0].shape
    rows = mix.shape[1]
    degrees = legendre.shape[2]
    return pl.pallas_call(
        legendre_kernel,
        grid=(slots,),
        in_specs=[
            pl.BlockSpec(memory_space=pltpu.SMEM),
            pl.BlockSpec(mix.shape, lambda i: (0, 0, 0)),
            pl.BlockSpec((1, lats, degrees), lambda i: (i, 0, 0)),
        ] + [pl.BlockSpec((1, width, lats), lambda i: (i, 0, 0))] * len(panels),
        out_specs=pl.BlockSpec((1, rows, degrees), lambda i: (i, 0, 0)),
        out_shape=jax.ShapeDtypeStruct((slots, rows, degrees), jnp.float32),
        compiler_params=params(),
        name="legendre",
    )(owners, mix, legendre, *panels)


def shards(bands, pairs, grid_fields, band_rows, wave_owner, lower_blocks, pivot_inverse, upper_blocks, legendre):
    slot_rows, columns, lons = grid_fields.shape
    lon_total = lons * 2 * pairs
    per, lats, _ = legendre.shape
    a, b = lax.axis_index("aa"), lax.axis_index("ba")
    side = b // 2
    half = columns // 2
    group = 2 * pairs

    grid = jnp.transpose(grid_fields, (1, 0, 2)).reshape(2, half, slot_rows, lons)
    duos = [[2 * y, 2 * y + 1] for y in range(pairs)]
    grid = lax.all_to_all(grid, "ba", split_axis=0, concat_axis=0, axis_index_groups=duos, tiled=True)

    owners = wave_owner.reshape(bands, pairs, 2, per)
    pad = -(2 * per) % 8
    rows = 2 * per + pad

    def side_rows(which):
        mine = lax.dynamic_index_in_dim(owners, which, 1, keepdims=False)
        waves = jnp.concatenate([mine, mine], axis=2)
        return jnp.pad(waves, ((0, 0), (0, 0), (0, pad))).reshape(-1)

    quadrant = jnp.asarray(np.tile(np.repeat(np.arange(2), per).tolist() + [0] * pad, bands * 2), jnp.int32)
    tables = [make_table(side_rows(w), quadrant, side * 2 * lons, 2 * lons, lon_total) for w in (1 - side, side)]

    ends = jnp.cumsum(band_rows)
    slot = jnp.arange(slot_rows, dtype=jnp.int32)
    target = jnp.where(slot[None, :] < band_rows[:, None], (ends - band_rows)[:, None] + slot[None, :], -1)
    place = (target[:, :, None] == jnp.arange(lats, dtype=jnp.int32)).astype(jnp.bfloat16)

    dests = 2 * bands
    count = half // CHUNKS
    across = [(2 * y + c, 2 * (1 - y) + c) for y in range(pairs) for c in range(2)]
    teams = [[aa * group + 2 * y + c for aa in range(bands) for c in range(2)] for y in range(pairs)]
    width = -(-4 * count // 16) * 16
    order = np.zeros((per * width, 2 * count * rows), np.float32)
    wide = np.full(CHUNKS * width, -1)
    for member in range(2):
        for q in range(count):
            for part in range(2):
                line = (part * 2 + member) * count + q
                for i in range(per):
                    order[i * width + line, (member * count + q) * rows + part * per + i] = 1
                for chunk in range(CHUNKS):
                    wide[chunk * width + line] = part * columns + member * half + chunk * count + q
    order = jnp.asarray(order, jnp.bfloat16)

    operator = vertical_operator(lower_blocks, pivot_inverse, upper_blocks)
    mix = jnp.kron(jnp.eye(2, dtype=jnp.float32), operator)
    mix = jnp.where(wide[None, :] >= 0, jnp.take(mix, np.maximum(wide, 0), axis=1), 0.0)
    high = mix.astype(jnp.bfloat16)
    low = (mix - high.astype(jnp.float32)).astype(jnp.bfloat16)
    mix = jnp.stack([high, low])

    parts = dft(tables[0], grid, 0, count, dests)
    sent = [lax.ppermute(parts, "ba", across)]
    placed = []
    for chunk in range(CHUNKS):
        came = sent[chunk]
        if chunk + 1 < CHUNKS:
            parts = dft(tables[0], grid, (chunk + 1) * count, count, dests)
            came, parts = lax.optimization_barrier((came, parts))
            sent.append(lax.ppermute(parts, "ba", across))
        if chunk >= 2:
            came, placed[chunk - 2] = lax.optimization_barrier((came, placed[chunk - 2]))
        full = dft(tables[1], grid, chunk * count, count, dests, came)
        arrived = lax.all_to_all(full, ("aa", "ba"), split_axis=0, concat_axis=0, axis_index_groups=teams, tiled=True)
        arrived = arrived.reshape(bands, 2 * count * rows, slot_rows)
        placed.append(place_rows(place, order, arrived, per))

    mine = lax.dynamic_slice_in_dim(wave_owner, (a * group + b) * per, per)
    return project(mine, mix, placed, legendre)


def solution(mesh):
    bands, group = mesh.shape["aa"], mesh.shape["ba"]
    placed = (P("aa", None, "ba"), P(), P(), P(), P(), P(), P(("aa", "ba"), None, None))
    return jax.shard_map(
        functools.partial(shards, bands, group // 2),
        mesh=mesh, in_specs=placed, out_specs=P(("aa", "ba"), None, None), check_vma=False,
    )
```

```python
import functools
import math

import jax
import jax.numpy as jnp
import numpy as np
from jax import lax
from jax.experimental import pallas as pl
from jax.experimental.pallas import tpu as pltpu
from jax.sharding import PartitionSpec as P

NT = 1279
CHUNKS = 6
VMEM = 48 * 1024 * 1024


def params():
    return pltpu.CompilerParams(vmem_limit_bytes=VMEM)


def angle(phase, lon_total):
    return phase.astype(jnp.float32) * (2.0 * math.pi / lon_total)


def table_kernel(base_ref, step_ref, out_ref, *, lon_total):
    base = angle(base_ref[...], lon_total)
    step = angle(step_ref[...], lon_total)
    cos_a, sin_a = jnp.cos(base), jnp.sin(base)
    cos_b, sin_b = jnp.cos(step), jnp.sin(step)
    for block in range(out_ref.shape[1] // 128):
        one = slice(block, block + 1)
        out_ref[:, block * 128:(block + 1) * 128] = (
            cos_a[:, one] * cos_b - sin_a[:, one] * sin_b
        ).astype(jnp.bfloat16)


def make_table(waves, quadrant, first_lon, lon_count, lon_total):
    rows = waves.shape[0]
    blocks = lon_count // 128
    starts = first_lon + 128 * jnp.arange(128, dtype=jnp.int32)
    base = (waves[:, None] * starts[None, :] + quadrant[:, None] * (lon_total // 4)) % lon_total
    step = (waves[:, None] * jnp.arange(128, dtype=jnp.int32)[None, :]) % lon_total
    tile = rows // 8 if rows % 64 == 0 else rows
    return pl.pallas_call(
        functools.partial(table_kernel, lon_total=lon_total),
        grid=(rows // tile,),
        in_specs=[pl.BlockSpec((tile, 128), lambda i: (i, 0))] * 2,
        out_specs=pl.BlockSpec((tile, blocks * 128), lambda i: (i, 0)),
        out_shape=jax.ShapeDtypeStruct((rows, blocks * 128), jnp.bfloat16),
        compiler_params=params(),
        name="table",
    )(base, step)


NN = (((1,), (1,)), ((), ()))


def dft_kernel(table_ref, grid_ref, *rest):
    out_ref = rest[-1]
    width = grid_ref.shape[3]
    dests, _, rows, _ = out_ref.shape
    total = lax.dot_general(table_ref[:, :width], grid_ref[0, 0], NN, preferred_element_type=jnp.float32)
    total += lax.dot_general(table_ref[:, width:], grid_ref[1, 0], NN, preferred_element_type=jnp.float32)
    for dest in range(dests):
        piece = total[dest * rows:(dest + 1) * rows]
        if len(rest) == 2:
            piece = piece + rest[0][dest, 0].astype(jnp.float32)
        out_ref[dest, 0] = piece.astype(jnp.bfloat16)


def dft(table, grid, first, count, dests, more=None):
    rows = table.shape[0] // dests
    slots = grid.shape[2]
    out_spec = pl.BlockSpec((dests, 1, rows, slots), lambda i: (0, i, 0, 0))
    in_specs = [
        pl.BlockSpec(table.shape, lambda i: (0, 0)),
        pl.BlockSpec((2, 1) + grid.shape[2:], lambda i: (0, first + i, 0, 0)),
    ]
    operands = [table, grid]
    if more is not None:
        in_specs.append(out_spec)
        operands.append(more)
    flops = 2 * table.shape[0] * table.shape[1] * slots * count
    return pl.pallas_call(
        dft_kernel,
        grid=(count,),
        in_specs=in_specs,
        out_specs=out_spec,
        out_shape=jax.ShapeDtypeStruct((dests, count, rows, slots), jnp.bfloat16),
        compiler_params=params(),
        cost_estimate=pl.CostEstimate(flops=flops, bytes_accessed=table.size * 2 + count * slots * 6000, transcendentals=0),
        name="dft",
    )(*operands)


def place_kernel(place_ref, order_ref, in_ref, out_ref):
    bands = in_ref.shape[0]
    slots, width, lats = out_ref.shape
    total = jnp.zeros((slots * width, lats), jnp.float32)
    for band in range(bands):
        ordered = jnp.dot(order_ref[...], in_ref[band], preferred_element_type=jnp.float32)
        total += jnp.dot(ordered.astype(jnp.bfloat16), place_ref[band], preferred_element_type=jnp.float32)
    out_ref[...] = total.astype(jnp.bfloat16).reshape(slots, width, lats)


def place_rows(place, order, arrived, slots):
    bands, rows, slot_rows = arrived.shape
    lats = place.shape[2]
    flops = 2 * order.shape[0] * bands * slot_rows * lats
    return pl.pallas_call(
        place_kernel,
        out_shape=jax.ShapeDtypeStruct((slots, order.shape[0] // slots, lats), jnp.bfloat16),
        in_specs=[pl.BlockSpec(memory_space=pltpu.VMEM)] * 3,
        out_specs=pl.BlockSpec(memory_space=pltpu.VMEM),
        compiler_params=params(),
        cost_estimate=pl.CostEstimate(flops=2 * flops, bytes_accessed=place.size * 2, transcendentals=0),
        name="place",
    )(place, order, arrived)


def solve_kernel(lower_ref, inverse_ref, upper_ref, out_ref, *, fields, levels):
    lane = lax.broadcasted_iota(jnp.int32, (1, 128), 1)
    cut = lambda ref, a, b, k: ref[(a * fields + b) * levels + k]

    def apply(ref, k, vector):
        return [sum(cut(ref, a, b, k) * vector[b] for b in range(fields)) for a in range(fields)]

    state = [jnp.zeros((1, 128), jnp.float32) for _ in range(fields)]
    sweeps = []
    for k in range(levels):
        low = apply(lower_ref, k, state)
        source = [(lane == f * levels + k).astype(jnp.float32) - low[f] for f in range(fields)]
        state = apply(inverse_ref, k, source)
        sweeps.append(state)
    state = [jnp.zeros((1, 128), jnp.float32) for _ in range(fields)]
    for k in range(levels - 1, -1, -1):
        back = apply(inverse_ref, k, apply(upper_ref, k, state))
        state = [sweeps[k][f] - back[f] for f in range(fields)]
        for f in range(fields):
            out_ref[f * levels + k:f * levels + k + 1, :] = state[f]


def vertical_operator(lower_blocks, pivot_inverse, upper_blocks):
    fields, _, levels = lower_blocks.shape
    whole = pl.pallas_call(
        functools.partial(solve_kernel, fields=fields, levels=levels),
        in_specs=[pl.BlockSpec(memory_space=pltpu.SMEM)] * 3,
        out_specs=pl.BlockSpec(memory_space=pltpu.VMEM),
        out_shape=jax.ShapeDtypeStruct((fields * levels, 128), jnp.float32),
        name="vertical",
    )(lower_blocks.reshape(-1), pivot_inverse.reshape(-1), upper_blocks.reshape(-1))
    return whole[:, :fields * levels]


def legendre_kernel(owner_ref, mix_ref, legendre_ref, *rest):
    out_ref = rest[-1]
    slot = pl.program_id(0)
    panel = jnp.concatenate([ref[0] for ref in rest[:-1]], axis=0)
    total = jnp.dot(mix_ref[...], jnp.concatenate([panel, panel], axis=0), preferred_element_type=jnp.float32)
    high = total.astype(jnp.bfloat16)
    low = (total - high.astype(jnp.float32)).astype(jnp.bfloat16)
    both = jnp.concatenate([high, low], axis=0)
    both = jnp.dot(both, legendre_ref[0], preferred_element_type=jnp.float32)
    count = total.shape[0]
    mixed = both[:count] + both[count:]
    degree = lax.broadcasted_iota(jnp.int32, mixed.shape, 1)
    out_ref[0] = jnp.where(degree + owner_ref[slot] <= NT, mixed, 0.0)


def project(owners, mix, panels, legendre):
    slots, width, lats = panels[0].shape
    rows = mix.shape[0]
    degrees = legendre.shape[2]
    return pl.pallas_call(
        legendre_kernel,
        grid=(slots,),
        in_specs=[
            pl.BlockSpec(memory_space=pltpu.SMEM),
            pl.BlockSpec(mix.shape, lambda i: (0, 0)),
            pl.BlockSpec((1, lats, degrees), lambda i: (i, 0, 0)),
        ] + [pl.BlockSpec((1, width, lats), lambda i: (i, 0, 0))] * len(panels),
        out_specs=pl.BlockSpec((1, rows, degrees), lambda i: (i, 0, 0)),
        out_shape=jax.ShapeDtypeStruct((slots, rows, degrees), jnp.float32),
        compiler_params=params(),
        name="legendre",
    )(owners, mix, legendre, *panels)


def shards(bands, pairs, grid_fields, band_rows, wave_owner, lower_blocks, pivot_inverse, upper_blocks, legendre):
    slot_rows, columns, lons = grid_fields.shape
    lon_total = lons * 2 * pairs
    per, lats, _ = legendre.shape
    a, b = lax.axis_index("aa"), lax.axis_index("ba")
    side = b // 2
    half = columns // 2
    group = 2 * pairs

    grid = jnp.transpose(grid_fields, (1, 0, 2)).reshape(2, half, slot_rows, lons)
    duos = [[2 * y, 2 * y + 1] for y in range(pairs)]
    grid = lax.all_to_all(grid, "ba", split_axis=0, concat_axis=0, axis_index_groups=duos, tiled=True)

    owners = wave_owner.reshape(bands, pairs, 2, per)
    pad = -(2 * per) % 8
    rows = 2 * per + pad

    def side_rows(which):
        mine = lax.dynamic_index_in_dim(owners, which, 1, keepdims=False)
        waves = jnp.concatenate([mine, mine], axis=2)
        return jnp.pad(waves, ((0, 0), (0, 0), (0, pad))).reshape(-1)

    quadrant = jnp.asarray(np.tile(np.repeat(np.arange(2), per).tolist() + [0] * pad, bands * 2), jnp.int32)
    tables = [make_table(side_rows(w), quadrant, side * 2 * lons, 2 * lons, lon_total) for w in (1 - side, side)]

    ends = jnp.cumsum(band_rows)
    slot = jnp.arange(slot_rows, dtype=jnp.int32)
    target = jnp.where(slot[None, :] < band_rows[:, None], (ends - band_rows)[:, None] + slot[None, :], -1)
    place = (target[:, :, None] == jnp.arange(lats, dtype=jnp.int32)).astype(jnp.bfloat16)

    dests = 2 * bands
    count = half // CHUNKS
    across = [(2 * y + c, 2 * (1 - y) + c) for y in range(pairs) for c in range(2)]
    teams = [[aa * group + 2 * y + c for aa in range(bands) for c in range(2)] for y in range(pairs)]
    width = -(-4 * count // 16) * 16
    order = np.zeros((per * width, 2 * count * rows), np.float32)
    wide = np.full(CHUNKS * width, -1)
    for member in range(2):
        for q in range(count):
            for part in range(2):
                line = (part * 2 + member) * count + q
                for i in range(per):
                    order[i * width + line, (member * count + q) * rows + part * per + i] = 1
                for chunk in range(CHUNKS):
                    wide[chunk * width + line] = part * columns + member * half + chunk * count + q
    order = jnp.asarray(order, jnp.bfloat16)

    operator = vertical_operator(lower_blocks, pivot_inverse, upper_blocks)
    mix = jnp.kron(jnp.eye(2, dtype=jnp.float32), operator)
    mix = jnp.where(wide[None, :] >= 0, jnp.take(mix, np.maximum(wide, 0), axis=1), 0.0)
    high = mix.astype(jnp.bfloat16)
    low = (mix - high.astype(jnp.float32)).astype(jnp.bfloat16)
    mix = jnp.concatenate([high, low], axis=1)

    parts = dft(tables[0], grid, 0, count, dests)
    sent = [lax.ppermute(parts, "ba", across)]
    placed = []
    for chunk in range(CHUNKS):
        came = sent[chunk]
        if chunk + 1 < CHUNKS:
            parts = dft(tables[0], grid, (chunk + 1) * count, count, dests)
            came, parts = lax.optimization_barrier((came, parts))
            sent.append(lax.ppermute(parts, "ba", across))
        if chunk >= 2:
            came, placed[chunk - 2] = lax.optimization_barrier((came, placed[chunk - 2]))
        full = dft(tables[1], grid, chunk * count, count, dests, came)
        arrived = lax.all_to_all(full, ("aa", "ba"), split_axis=0, concat_axis=0, axis_index_groups=teams, tiled=True)
        arrived = arrived.reshape(bands, 2 * count * rows, slot_rows)
        placed.append(place_rows(place, order, arrived, per))

    mine = lax.dynamic_slice_in_dim(wave_owner, (a * group + b) * per, per)
    return project(mine, mix, placed, legendre)


def solution(mesh):
    bands, group = mesh.shape["aa"], mesh.shape["ba"]
    placed = (P("aa", None, "ba"), P(), P(), P(), P(), P(), P(("aa", "ba"), None, None))
    return jax.shard_map(
        functools.partial(shards, bands, group // 2),
        mesh=mesh, in_specs=placed, out_specs=P(("aa", "ba"), None, None), check_vma=False,
    )
```
